32 devices in a mesh: member: 4 (over z), tile: 8 (over y, x, core).
Axes of the slice: x: 2, y: 2, z: 4, core: 2. Of those that a mesh axis runs over, the one named last changes fastest.
Arguments:
- adjoint_final: bfloat16 [4, 32, 256, 192], P('member', None, 'tile'), may hold values from -6 to 6
- states: bfloat16 [2, 4, 32, 256, 192], P(None, 'member', None, 'tile'), may hold values from -12 to 12
- kernel: float32 [7, 7, 192], replicated, may hold values from -0.875 to 0.875
- norm_gain: float32 [192], replicated, may hold values from 0.1 to 1.9
- up_weight: bfloat16 [192, 768], replicated, may hold values from -0.4375 to 0.4375
- up_bias: float32 [768], replicated, may hold values from -4 to 4
- down_weight: bfloat16 [768, 192], replicated, may hold values from -0.21875 to 0.21875
- obs_cell: int32 [2, 8, 8, 16], P(None, 'tile'), may hold values from 0 to 127
- obs_count: int32 [2, 8, 8], P(None, 'tile'), may hold values from 1 to 16, 64 in all within a row
- obs_value: bfloat16 [2, 8, 8, 16, 192], P(None, 'tile'), may hold values from -6 to 6
- obs_error: bfloat16 [2, 8, 8, 16], P(None, 'tile'), may hold values from 0.099609375 to 1
Outputs:
- adjoint_initial: bfloat16 [4, 32, 256, 192], P('member', None, 'tile')
The draws below stay inside these ranges and needn't reach their ends.
Inputs may be any that keep to these rules, and one draw needn't show every extreme that they name: `obs_cell`: a cell number is latitude offset within the band times 32 plus longitude offset within the tile. `obs_count`: the counts of one band and time add up to 64, and the largest of them is 16.
All inputs are finite; a program needn't handle non-finite values.
Results may differ from the reference program's by a relative error of at most 0.006.
Values may be sent and summed in bfloat16 or wider, within the bound.
A program may use at most 64 MiB of HBM per device.

```python
import math
import jax
import jax.numpy as jnp
import numpy as np
from jax import lax

C = 192
HID = 768
STEPS = 2
LAT = 32
LON_DEV = 32
CAP = 16
MEMBERS = 4
NLON = 256
BAND = 4
N_TILE = 8


def draw_states(key, part):
    base_key, chan_key, member_key, noise_key = jax.random.split(jax.random.fold_in(key, 7), 4)
    full_shape = (STEPS, MEMBERS, LAT, NLON, C)
    base_field = jax.random.normal(base_key, (STEPS, 1, LAT, NLON, C), jnp.float32)
    chan_scale = jnp.exp(jax.random.uniform(chan_key, (C,), jnp.float32, math.log(0.3), math.log(2.0)))
    noise_part = jax.random.normal(noise_key, full_shape, jnp.float32)
    member_scale = jnp.exp(jax.random.uniform(member_key, (1, MEMBERS, 1, 1, 1), jnp.float32, math.log(0.4), math.log(4.0)))
    return jnp.clip(base_field + chan_scale * member_scale * noise_part, -12.0, 12.0).astype(jnp.bfloat16)


def place_ends(drawn, own_key, low, top_value):
    spot = [jax.random.randint(jax.random.fold_in(own_key, axis), (), 0, length) for axis, length in enumerate(drawn.shape)]
    main_axis = drawn.shape.index(max(drawn.shape))
    neighbour = spot[:main_axis] + [(spot[main_axis] + 1) % drawn.shape[main_axis]] + spot[main_axis + 1:]
    return drawn.at[tuple(spot)].set(low).at[tuple(neighbour)].set(top_value)


def block_scale(key, extent, pieces, low, high):
    loudness = 1.0
    for dim, parts in pieces:
        heights = jax.random.uniform(jax.random.fold_in(jax.random.fold_in(key, 6), dim), (parts,), jnp.float32, low / len(pieces), high / len(pieces))
        loudness = loudness * jnp.repeat(jnp.exp(heights), extent[dim] // parts).reshape((-1,) + (1,) * (len(extent) - 1 - dim))
    return loudness


def profile(count, total, bound, lean):
    loads = [(1 << 20) // math.isqrt(rank ** lean) + 1 for rank in range(2, count + 1)]
    spare, given = total - bound - (count - 1), [1] * (count - 1)
    while spare > 0:
        free = [i for i in range(count - 1) if given[i] < bound]
        pool, remaining = sum([loads[i] for i in free]), spare
        for i in free:
            addition = min(bound - given[i], max(1, remaining * loads[i] // pool), spare)
            given[i] = given[i] + addition
            spare = spare - addition
    return np.array([bound] + given)


def ragged_sizes(own_key, amount, total, reach, slope):
    if amount == 2:
        one = jax.random.randint(own_key, (), max(1, total - reach), min(reach, total - 1) + 1)
        return jnp.stack([one, total - one])
    tallies = jnp.asarray(profile(amount, total, reach, slope), jnp.int32)
    couples = (amount - 1) // 2
    source_of, taker = tallies[1:1 + 2 * couples:2], tallies[2:2 + 2 * couples:2]
    room = jnp.minimum(source_of - 1, reach - taker)
    shifted = jax.random.randint(jax.random.fold_in(own_key, 1), (couples,), 0, 1 << 20) % (room + 1)
    tallies = tallies.at[1:1 + 2 * couples:2].set(source_of - shifted).at[2:2 + 2 * couples:2].set(taker + shifted)
    return tallies[jax.random.permutation(jax.random.fold_in(own_key, 2), amount)]


def gaussian(key, extent, scale, reach, cuts=(), kind=jnp.bfloat16):
    entries = jax.random.normal(key, extent, jnp.float32) * scale
    if len(cuts) > 0:
        entries = block_scale(key, extent, cuts, -0.22, 0.18) * entries
    return jnp.clip(entries, min=-reach, max=reach).astype(kind)


def setup_inputs(seed: int = 0) -> dict:
    streams_of = jax.random.split(jax.random.key(seed), 12)
    return {
        "adjoint_final": gaussian(streams_of[0], (MEMBERS, LAT, NLON, C), 1.0, 6.0, ((0, 4), (2, 8))),
        "states": draw_states(jax.random.fold_in(streams_of[11], 71), 0),
        "kernel": gaussian(streams_of[2], (7, 7, C), 49 ** -0.5, 0.875, (), jnp.float32),
        "norm_gain": jnp.clip(1.0 + 0.18 * jax.random.normal(streams_of[3], (C,), jnp.float32), 0.1, 1.9),
        "up_weight": gaussian(streams_of[4], (C, HID), C ** -0.5, 0.4375),
        "up_bias": gaussian(streams_of[5], (HID,), 1.0, 4.0, (), jnp.float32),
        "down_weight": gaussian(streams_of[6], (HID, C), HID ** -0.5, 0.21875),
        "obs_cell": place_ends(jax.random.randint(streams_of[7], (STEPS, N_TILE, N_TILE, CAP), 0, BAND * LON_DEV), jax.random.fold_in(streams_of[7], 1), 0, (BAND * LON_DEV) - 1).astype(jnp.int32),
        "obs_count": jax.vmap(lambda own: ragged_sizes(own, N_TILE, N_TILE * CAP // 2, CAP, 2))(jax.random.split(streams_of[8], STEPS * N_TILE)).reshape((STEPS, N_TILE, N_TILE)).astype(jnp.int32),
        "obs_value": gaussian(streams_of[9], (STEPS, N_TILE, N_TILE, CAP, C), 1.0, 6.0, ((1, 8),)),
        "obs_error": jnp.clip(jnp.exp(math.log(1.0) - 2.306499 * jax.random.uniform(streams_of[10], (STEPS, N_TILE, N_TILE, CAP), jnp.float32) ** block_scale(streams_of[10], (STEPS, N_TILE, N_TILE, CAP), ((1, 8),), -0.2, 0.2)), 0.099609375, 1.0).astype(jnp.bfloat16),
    }


slope_coef = math.sqrt(2.0 / math.pi)
cubic_coef = 0.044715
norm_eps = 1e-06

def gelu_slope(preact):
    inner_arg = slope_coef * (preact + cubic_coef * preact * preact * preact)
    tanh_val = jnp.tanh(inner_arg)
    return 0.5 * (1.0 + tanh_val) + 0.5 * preact * (1.0 - tanh_val * tanh_val) * slope_coef * (1.0 + 3.0 * cubic_coef * preact * preact)

def wrap_lon(field_in):
    return jnp.concatenate([field_in[:, -3:], field_in, field_in[:, :3]], axis=1)

def pad_rows(field_in):
    return jnp.pad(field_in, ((3, 3), (0, 0), (0, 0)))

def depthwise(padded, kernel, lat_count, lon_width):
    summed = jnp.zeros((lat_count, lon_width, padded.shape[2]), jnp.float32)
    for row_tap in range(7):
        for col_tap in range(7):
            summed = summed + kernel[row_tap, col_tap] * padded[row_tap:row_tap + lat_count, col_tap:col_tap + lon_width]
    return summed

def depthwise_adjoint(padded, kernel, lat_count, lon_width):
    summed = jnp.zeros((lat_count, lon_width, padded.shape[2]), jnp.float32)
    for row_tap in range(7):
        for col_tap in range(7):
            summed = summed + kernel[row_tap, col_tap] * padded[6 - row_tap:6 - row_tap + lat_count, 6 - col_tap:6 - col_tap + lon_width]
    return summed

def member_step(adjoint, state, forcing, kernel, norm_gain, up_weight, up_bias, down_weight):
    lat_count, lon_width, channels = state.shape
    hidden = depthwise(pad_rows(wrap_lon(state.astype(jnp.float32))), kernel, lat_count, lon_width)
    centred = hidden - lax.optimization_barrier(jnp.mean(hidden, axis=-1, keepdims=True))
    inv_std = lax.rsqrt(lax.optimization_barrier(jnp.mean(centred * centred, axis=-1, keepdims=True)) + norm_eps)
    unit_norm = centred * inv_std
    normed = (unit_norm * norm_gain).astype(jnp.bfloat16)
    preact = jnp.dot(normed.reshape(-1, channels), up_weight, preferred_element_type=jnp.float32) + up_bias
    adj_act = jnp.dot(adjoint.reshape(-1, channels), down_weight.T, preferred_element_type=jnp.float32)
    adj_pre = (adj_act * gelu_slope(preact)).astype(jnp.bfloat16)
    adj_norm = jnp.dot(adj_pre, up_weight.T, preferred_element_type=jnp.float32).reshape(state.shape)
    scaled = adj_norm * norm_gain
    adj_hidden = (inv_std * (scaled - lax.optimization_barrier(jnp.mean(scaled, axis=-1, keepdims=True)) - unit_norm * lax.optimization_barrier(jnp.mean(scaled * unit_norm, axis=-1, keepdims=True)))).astype(jnp.bfloat16)
    spread_back = depthwise_adjoint(pad_rows(wrap_lon(adj_hidden.astype(jnp.float32))), kernel, lat_count, lon_width)
    return (adjoint.astype(jnp.float32) + spread_back + forcing).astype(jnp.bfloat16)

def reference(adjoint_final, states, kernel, norm_gain, up_weight, up_bias, down_weight, obs_cell, obs_count, obs_value, obs_error):
    band_ids = jnp.arange(N_TILE, dtype=jnp.int32)[:, None, None]
    tile_ids = jnp.arange(N_TILE, dtype=jnp.int32)[None, :, None]
    adjoint = adjoint_final
    for section_idx in range(STEPS):
        cell_ids = obs_cell[section_idx]
        lat_ids = band_ids * BAND + cell_ids // LON_DEV
        lon_ids = tile_ids * LON_DEV + cell_ids % LON_DEV
        live_mask = jnp.arange(CAP, dtype=jnp.int32)[None, None, :] < obs_count[section_idx][:, :, None]
        sampled = states[section_idx][:, lat_ids, lon_ids, :].astype(jnp.float32)
        ens_mean = lax.optimization_barrier(jnp.sum(sampled, axis=0)) / MEMBERS
        ens_var = lax.optimization_barrier(jnp.sum(sampled * sampled, axis=0)) / MEMBERS - ens_mean * ens_mean
        ratio = (sampled - obs_value[section_idx].astype(jnp.float32)) / (obs_error[section_idx].astype(jnp.float32)[..., None] + ens_var)
        dep_rows = jnp.where(live_mask[None, :, :, :, None], ratio, 0.0).astype(jnp.bfloat16)

        def per_member(packed):
            adjoint_m, state_m, rows_m = packed
            forcing = jnp.zeros((LAT, NLON, C), jnp.float32).at[lat_ids, lon_ids].add(rows_m.astype(jnp.float32))
            return member_step(adjoint_m, state_m, forcing, kernel, norm_gain, up_weight, up_bias, down_weight)
        adjoint = lax.map(per_member, (adjoint, states[section_idx], dep_rows))
    return adjoint
```

```python
import functools
import math

import jax
import jax.numpy as jnp
from jax import lax
from jax.experimental import pallas as pl
from jax.experimental.pallas import tpu as pltpu
from jax.sharding import PartitionSpec as P

slope_coef = math.sqrt(2.0 / math.pi)
cubic_coef = 0.044715
norm_eps = 1e-06
MESH = pl.DeviceIdType.MESH
F32, BF16 = jnp.float32, jnp.bfloat16
GROUP = 4
PAD = 8


def gelu_slope(u):
    u2 = u * u
    w = jnp.tanh(u * (slope_coef + (slope_coef * cubic_coef) * u2))
    outer = u * (0.5 * slope_coef + (1.5 * slope_coef * cubic_coef) * u2)
    return (0.5 + 0.5 * w) + (1.0 - w * w) * outer


def kernel(
    tiles, members, adj_ref, st_ref, kern_ref, gain_ref, up_ref, bias_ref, down_ref, pack_ref, out_ref,
    xb, ahb, cur, plane0, plane1, kbr, hbuf, turn, upt, downt, orecv, samp, dep,
    obs_send, obs_recv, mem_send, mem_recv, halo_send, halo_recv,
):
    steps, lat, lon, chan = st_ref.shape
    half, cells, slots = lon // 2, lat * lon, tiles * pack_ref.shape[2]
    rest = chan - 128
    pitch = turn.shape[1] // lon
    rows = GROUP * lat
    t, m = lax.axis_index("tile"), lax.axis_index("member")

    barrier = pltpu.get_barrier_semaphore()
    for d in range(1, tiles):
        pl.semaphore_signal(barrier, inc=1, device_id={"tile": lax.rem(t + d, tiles)}, device_id_type=MESH)
    for d in range(1, members):
        pl.semaphore_signal(barrier, inc=1, device_id={"member": lax.rem(m + d, members)}, device_id_type=MESH)

    def to_lon_major(load, store):
        for i in range(lat):
            v = load(i).astype(F32)
            turn[0, pl.ds(i * pitch, lon), :] = v[:, :128]
            turn[1, pl.ds(i * pitch, lon), :rest] = v[:, 128:]
        for k in range(lon):
            a = turn[0, pl.ds(k, lat, stride=pitch), :]
            b = turn[1, pl.ds(k, lat, stride=pitch), :]
            store(k, a, b[:, :rest])

    def halo_copies(buf, s, n):
        right, left = lax.rem(t + 1, tiles), lax.rem(t + tiles - 1, tiles)
        out = []
        for d, (src, dst, to) in enumerate(((lon, 0, right), (3, lon + 3, left))):
            out.append(pltpu.make_async_remote_copy(
                src_ref=buf.at[s, pl.ds(src, 3)], dst_ref=buf.at[s, pl.ds(dst, 3)],
                send_sem=halo_send.at[n, d], recv_sem=halo_recv.at[n, d],
                device_id={"tile": to}, device_id_type=MESH))
        return out

    for s in range(steps):
        def store_x(k, a, b, s=s):
            xb[s, 3 + k, :, :128] = a.astype(BF16)
            xb[s, 3 + k, :, 128:] = b.astype(BF16)
        to_lon_major(lambda i, s=s: st_ref[s, i], store_x)

    pl.semaphore_wait(barrier, tiles - 1 + members - 1)
    obs = []
    for d in range(1, tiles):
        to = lax.rem(t + d, tiles)
        obs.append(pltpu.make_async_remote_copy(
            src_ref=pack_ref.at[to], dst_ref=orecv.at[t], send_sem=obs_send.at[d], recv_sem=obs_recv.at[d],
            device_id={"tile": to}, device_id_type=MESH))
        obs[-1].start()
    halos = [halo_copies(xb, s, s) for s in range(steps)]
    for pair in halos:
        for c in pair:
            c.start()
    orecv[pl.ds(t, 1)] = pack_ref[pl.ds(t, 1)]

    def store_adj(k, a, b):
        cur[k, :, :128] = a.astype(BF16)
        cur[k, :, 128:] = b.astype(BF16)
    to_lon_major(lambda i: adj_ref[i], store_adj)
    upt[...] = up_ref[...].T
    downt[...] = down_ref[...].T
    for n in range(49):
        kbr[0, n] = jnp.broadcast_to(kern_ref[n:n + 1, :128], (8, 128))
        tail = jnp.broadcast_to(kern_ref[n:n + 1, 128:], (8, rest))
        kbr[1, n, :, :rest] = tail
        kbr[1, n, :, rest:] = tail
    for plane in (plane0, plane1):
        plane[:, :PAD] = jnp.zeros((plane.shape[0], PAD, 128), F32)
        plane[:, PAD + lat:] = jnp.zeros((plane.shape[0], PAD, 128), F32)

    for c in obs:
        c.wait()

    def places(s):
        meta = orecv[:, s, :, 128:].astype(F32).reshape(slots, 128)
        lon_at, lat_at = meta[:, rest:rest + 1], meta[:, rest + 1:rest + 2]
        return meta, lon_at * lat + lat_at

    for s in range(steps):
        _, place = places(s)
        ids = lax.broadcasted_iota(jnp.int32, (slots, cells), 1).astype(F32)
        pick = jnp.where(ids == place, 1.0, 0.0).astype(BF16)
        got = jnp.dot(pick, xb[s, 3:3 + lon].reshape(cells, chan), preferred_element_type=F32)
        samp[pl.ds(m, 1), s] = got.astype(BF16).reshape(1, slots, chan)
    mem = []
    for d in range(1, members):
        mem.append(pltpu.make_async_remote_copy(
            src_ref=samp.at[m], dst_ref=samp.at[m], send_sem=mem_send.at[d], recv_sem=mem_recv.at[d],
            device_id={"member": lax.rem(m + d, members)}, device_id_type=MESH))
        mem[-1].start()

    def build(buf, s, wait):
        def put0(i, _):
            plane0[i, PAD:PAD + lat, :] = buf[s, i, :, :128].astype(F32)
            return 0

        def put1(i, _):
            plane1[i, PAD:PAD + lat, :] = jnp.concatenate(
                [buf[s, i, :, 128:].astype(F32), buf[s, i + half, :, 128:].astype(F32)], axis=-1)
            return 0
        lax.fori_loop(3, lon + 3, put0, 0)
        lax.fori_loop(3, half + 3, put1, 0)
        wait()
        for lo in (0, lon + 3):
            lax.fori_loop(lo, lo + 3, put0, 0)
        for lo in (0, half + 3):
            lax.fori_loop(lo, lo + 3, put1, 0)

    def conv_group(plane, p_id, first, flip):
        acc = [None] * GROUP
        for p in range(7):
            for r in range(GROUP + 6):
                v = plane[first + r, pl.ds(PAD - 3 + p, lat), :].reshape(lat // 8, 8, 128)
                for q in range(7):
                    o = r - q
                    if 0 <= o < GROUP:
                        n = (6 - p) * 7 + (6 - q) if flip else p * 7 + q
                        term = kbr[p_id, n][None] * v
                        acc[o] = term if acc[o] is None else acc[o] + term
        return jnp.concatenate([a.reshape(lat, 128) for a in acc], axis=0)

    def conv(i0, flip):
        hbuf[:rows, :128] = conv_group(plane0, 0, i0, flip)
        hbuf[rows:, :128] = conv_group(plane0, 0, half + i0, flip)
        both = conv_group(plane1, 1, i0, flip)
        hbuf[:rows, 128:] = both[:, :rest]
        hbuf[rows:, 128:] = both[:, rest:]
        return hbuf[...]

    def current(i0):
        return jnp.concatenate(
            [cur[pl.ds(i0, GROUP)].reshape(rows, chan), cur[pl.ds(half + i0, GROUP)].reshape(rows, chan)], axis=0)

    blocks = half // GROUP
    for s in range(steps):
        def wait_x(s=s):
            for c in halos[s]:
                c.wait()
        build(xb, s, wait_x)
        back = halo_copies(ahb, s, steps + s)

        def point(k, _, s=s, back=back):
            i0 = lax.rem(k * (blocks - 1), blocks) * GROUP
            hidden = conv(i0, False)
            centred = hidden - jnp.mean(hidden, axis=-1, keepdims=True)
            inv_std = lax.rsqrt(jnp.mean(centred * centred, axis=-1, keepdims=True) + norm_eps)
            unit = centred * inv_std
            normed = (unit * gain_ref[...]).astype(BF16)
            pre = jnp.dot(normed, up_ref[...], preferred_element_type=F32) + bias_ref[...]
            act = jnp.dot(current(i0), downt[...], preferred_element_type=F32)
            adj_pre = (act * gelu_slope(pre)).astype(BF16)
            scaled = jnp.dot(adj_pre, upt[...], preferred_element_type=F32) * gain_ref[...]
            ah = inv_std * (
                scaled - jnp.mean(scaled, axis=-1, keepdims=True)
                - unit * jnp.mean(scaled * unit, axis=-1, keepdims=True))
            ah = ah.astype(BF16)
            ahb[s, pl.ds(3 + i0, GROUP)] = ah[:rows].reshape(GROUP, lat, chan)
            ahb[s, pl.ds(3 + half + i0, GROUP)] = ah[rows:].reshape(GROUP, lat, chan)

            @pl.when(k == 1)
            def _():
                for c in back:
                    c.start()
            return 0
        lax.fori_loop(0, blocks, point, 0)

        if s == 0:
            for c in mem:
                c.wait()
            for z in range(steps):
                meta, _ = places(z)
                total = squares = None
                for i in range(members):
                    v = samp[i, z].astype(F32)
                    total = v if total is None else total + v
                    squares = v * v if squares is None else squares + v * v
                mean = total / members
                var = squares / members - mean * mean
                own = samp[pl.ds(m, 1), z].astype(F32).reshape(slots, chan)
                value = orecv[:, z, :, :chan].astype(F32).reshape(slots, chan)
                ratio = (own - value) / (meta[:, rest + 2:rest + 3] + var)
                dep[z] = jnp.where(meta[:, rest + 3:rest + 4] > 0.5, ratio, 0.0).astype(BF16)

        def wait_back(back=back):
            for c in back:
                c.wait()
        build(ahb, s, wait_back)
        _, place = places(s)
        line = jnp.broadcast_to(place, (slots, 128)).T[0:1, :]

        def spread(k, _, s=s, line=line):
            i0 = k * GROUP
            back_out = conv(i0, True)
            row = lax.broadcasted_iota(jnp.int32, (2 * rows, slots), 0)
            row = jnp.where(row < rows, row, row + (half * lat - rows)) + i0 * lat
            hit = jnp.where(row.astype(F32) == line, 1.0, 0.0).astype(BF16)
            forcing = jnp.dot(hit, dep[s], preferred_element_type=F32)
            new = current(i0).astype(F32) + back_out + forcing
            if s < steps - 1:
                new = new.astype(BF16)
                cur[pl.ds(i0, GROUP)] = new[:rows].reshape(GROUP, lat, chan)
                cur[pl.ds(half + i0, GROUP)] = new[rows:].reshape(GROUP, lat, chan)
            else:
                for g in range(2 * GROUP):
                    at = (i0 + (g // GROUP) * half + g % GROUP) * pitch
                    part = new[g * lat:(g + 1) * lat]
                    turn[0, pl.ds(at, lat), :] = part[:, :128]
                    turn[1, pl.ds(at, lat), :rest] = part[:, 128:]
            return 0
        lax.fori_loop(0, blocks, spread, 0)

    for i in range(lat):
        out_ref[i, :, :128] = turn[0, pl.ds(i, lon, stride=pitch), :].astype(BF16)
        out_ref[i, :, 128:] = turn[1, pl.ds(i, lon, stride=pitch), :][:, :rest].astype(BF16)


def per_device(
    adjoint_final, states, kernel_w, norm_gain, up_weight, up_bias, down_weight,
    obs_cell, obs_count, obs_value, obs_error,
):
    tiles, members = lax.axis_size("tile"), lax.axis_size("member")
    steps, _, lat, lon, chan = states.shape
    hid, cap = up_weight.shape[1], obs_cell.shape[3]
    band = lat // tiles
    cell = obs_cell[:, 0]
    slot = jnp.arange(cap, dtype=jnp.int32)
    meta = jnp.stack([
        (cell % lon).astype(BF16),
        (cell // lon + lax.axis_index("tile") * band).astype(BF16),
        obs_error[:, 0],
        (slot < obs_count[:, 0][..., None]).astype(BF16)], axis=-1)
    pack = jnp.concatenate([obs_value[:, 0], jnp.pad(meta, ((0, 0),) * 3 + ((0, 256 - chan - 4),))], axis=-1)
    pack = jnp.swapaxes(pack, 0, 1)
    slots = tiles * cap
    pitch = lat + 1
    vm = pl.BlockSpec(memory_space=pltpu.VMEM)
    out = pl.pallas_call(
        functools.partial(kernel, tiles, members),
        out_shape=jax.ShapeDtypeStruct((lat, lon, chan), BF16),
        in_specs=[vm] * 8,
        out_specs=vm,
        scratch_shapes=[
            pltpu.VMEM((steps, lon + 6, lat, chan), BF16),
            pltpu.VMEM((steps, lon + 6, lat, chan), BF16),
            pltpu.VMEM((lon, lat, chan), BF16),
            pltpu.VMEM((lon + 6, lat + 2 * PAD, 128), F32),
            pltpu.VMEM((lon // 2 + 6, lat + 2 * PAD, 128), F32),
            pltpu.VMEM((2, 49, 8, 128), F32),
            pltpu.VMEM((2 * GROUP * lat, chan), F32),
            pltpu.VMEM((2, pitch * lon, 128), F32),
            pltpu.VMEM((hid, chan), BF16),
            pltpu.VMEM((chan, hid), BF16),
            pltpu.VMEM((tiles, steps, cap, 256), BF16),
            pltpu.VMEM((members, steps, slots, chan), BF16),
            pltpu.VMEM((steps, slots, chan), BF16),
            pltpu.SemaphoreType.DMA((tiles,)),
            pltpu.SemaphoreType.DMA((tiles,)),
            pltpu.SemaphoreType.DMA((members,)),
            pltpu.SemaphoreType.DMA((members,)),
            pltpu.SemaphoreType.DMA((2 * steps, 2)),
            pltpu.SemaphoreType.DMA((2 * steps, 2)),
        ],
        compiler_params=pltpu.CompilerParams(
            collective_id=0, has_side_effects=True, vmem_limit_bytes=48 * 1024 * 1024),
    )(
        adjoint_final[0], states[:, 0], kernel_w.reshape(49, chan), norm_gain.reshape(1, chan),
        up_weight, up_bias.reshape(1, hid), down_weight, pack,
    )
    return out[None]


def solution(mesh):
    placed = (
        P("member", None, "tile", None),
        P(None, "member", None, "tile", None),
        P(), P(), P(), P(), P(),
        P(None, "tile", None, None),
        P(None, "tile", None),
        P(None, "tile", None, None, None),
        P(None, "tile", None, None),
    )
    return jax.shard_map(
        per_device, mesh=mesh, in_specs=placed, out_specs=P("member", None, "tile", None), check_vma=False)
```

```python
import functools
import math

import jax
import jax.numpy as jnp
from jax import lax
from jax.experimental import pallas as pl
from jax.experimental.pallas import tpu as pltpu
from jax.sharding import PartitionSpec as P

slope_coef = math.sqrt(2.0 / math.pi)
cubic_coef = 0.044715
norm_eps = 1e-06
MESH = pl.DeviceIdType.MESH
F32, BF16 = jnp.float32, jnp.bfloat16
GROUP = 4
PAD = 8


def gelu_slope(u):
    u2 = u * u
    w = jnp.tanh(u * (slope_coef + (slope_coef * cubic_coef) * u2))
    outer = u * (0.5 * slope_coef + (1.5 * slope_coef * cubic_coef) * u2)
    return (0.5 + 0.5 * w) + (1.0 - w * w) * outer


def kernel(
    tiles, members, adj_hbm, st_hbm, kern_hbm, gain_hbm, up_hbm, bias_hbm, down_hbm, obs_hbm, meta_ref, out_ref,
    adj_ref, st_ref, kern_ref, gain_ref, up_ref, bias_ref, downt, obs_ref, pack_ref,
    xb, ahb, cur, plane0, plane1, kbr, hbuf, turn, upt, orecv, samp, dep, local_sem,
    obs_send, obs_recv, mem_send, mem_recv, halo_send, halo_recv,
):
    steps, lat, lon, chan = st_ref.shape
    half, cells, slots = lon // 2, lat * lon, tiles * pack_ref.shape[2]
    rest = chan - 128
    pitch = turn.shape[1] // lon
    rows = GROUP * lat
    t, m = lax.axis_index("tile"), lax.axis_index("member")

    loads = []
    for src, dst in (
        (obs_hbm, obs_ref), *((st_hbm.at[s], st_ref.at[s]) for s in range(steps)), (kern_hbm, kern_ref),
        (up_hbm, up_ref), (adj_hbm, adj_ref), (down_hbm, downt), (gain_hbm, gain_ref), (bias_hbm, bias_ref),
    ):
        loads.append(pltpu.make_async_copy(src, dst, local_sem.at[len(loads)]))
        loads[-1].start()
    obs_load, st_loads, other_loads = loads[0], loads[1:1 + steps], loads[1 + steps:]

    barrier = pltpu.get_barrier_semaphore()
    for d in range(1, tiles):
        pl.semaphore_signal(barrier, inc=1, device_id={"tile": lax.rem(t + d, tiles)}, device_id_type=MESH)
    for d in range(1, members):
        pl.semaphore_signal(barrier, inc=1, device_id={"member": lax.rem(m + d, members)}, device_id_type=MESH)

    def to_lon_major(load, store):
        for i in range(lat):
            v = load(i).astype(F32)
            turn[0, pl.ds(i * pitch, lon), :] = v[:, :128]
            turn[1, pl.ds(i * pitch, lon), :rest] = v[:, 128:]
        for k in range(lon):
            a = turn[0, pl.ds(k, lat, stride=pitch), :]
            b = turn[1, pl.ds(k, lat, stride=pitch), :]
            store(k, a, b[:, :rest])

    def halo_copies(buf, s, n):
        right, left = lax.rem(t + 1, tiles), lax.rem(t + tiles - 1, tiles)
        out = []
        for d, (src, dst, to) in enumerate(((lon, 0, right), (3, lon + 3, left))):
            out.append(pltpu.make_async_remote_copy(
                src_ref=buf.at[s, pl.ds(src, 3)], dst_ref=buf.at[s, pl.ds(dst, 3)],
                send_sem=halo_send.at[n, d], recv_sem=halo_recv.at[n, d],
                device_id={"tile": to}, device_id_type=MESH))
        return out

    def turn_state(s):
        def store_x(k, a, b):
            xb[s, 3 + k, :, :128] = a.astype(BF16)
            xb[s, 3 + k, :, 128:] = b.astype(BF16)
        st_loads[s].wait()
        to_lon_major(lambda i: st_ref[s, i], store_x)

    obs_load.wait()
    for s in range(steps):
        pack_ref[:, s, :, :chan] = obs_ref[s]
        pack_ref[:, s, :, chan:] = meta_ref[s]
    orecv[pl.ds(t, 1)] = pack_ref[pl.ds(t, 1)]
    turn_state(0)

    pl.semaphore_wait(barrier, tiles - 1 + members - 1)
    obs = []
    for d in range(1, tiles):
        to = lax.rem(t + d, tiles)
        obs.append(pltpu.make_async_remote_copy(
            src_ref=pack_ref.at[to], dst_ref=orecv.at[t], send_sem=obs_send.at[d], recv_sem=obs_recv.at[d],
            device_id={"tile": to}, device_id_type=MESH))
        obs[-1].start()
    halos = [halo_copies(xb, s, s) for s in range(steps)]
    for s in range(steps):
        if s > 0:
            turn_state(s)
        for c in halos[s]:
            c.start()
    for c in other_loads:
        c.wait()

    def store_adj(k, a, b):
        cur[k, :, :128] = a.astype(BF16)
        cur[k, :, 128:] = b.astype(BF16)
    to_lon_major(lambda i: adj_ref[i], store_adj)
    upt[...] = up_ref[...].T
    for n in range(49):
        taps = kern_ref[n // 7, n % 7:n % 7 + 1, :]
        kbr[0, n] = jnp.broadcast_to(taps[:, :128], (8, 128))
        tail = jnp.broadcast_to(taps[:, 128:], (8, rest))
        kbr[1, n, :, :rest] = tail
        kbr[1, n, :, rest:] = tail
    for plane in (plane0, plane1):
        plane[:, :PAD] = jnp.zeros((plane.shape[0], PAD, 128), F32)
        plane[:, PAD + lat:] = jnp.zeros((plane.shape[0], PAD, 128), F32)

    for c in obs:
        c.wait()

    def places(s):
        meta = orecv[:, s, :, 128:].astype(F32).reshape(slots, 128)
        lon_at, lat_at = meta[:, rest:rest + 1], meta[:, rest + 1:rest + 2]
        return meta, lon_at * lat + lat_at

    mem = []
    for s in range(steps):
        _, place = places(s)
        ids = lax.broadcasted_iota(jnp.int32, (slots, cells), 1).astype(F32)
        pick = jnp.where(ids == place, 1.0, 0.0).astype(BF16)
        got = jnp.dot(pick, xb[s, 3:3 + lon].reshape(cells, chan), preferred_element_type=F32)
        samp[pl.ds(m, 1), s] = got.astype(BF16).reshape(1, slots, chan)
        mem.append([])
        for d in range(1, members):
            mem[s].append(pltpu.make_async_remote_copy(
                src_ref=samp.at[m, s], dst_ref=samp.at[m, s], send_sem=mem_send.at[s, d], recv_sem=mem_recv.at[s, d],
                device_id={"member": lax.rem(m + d, members)}, device_id_type=MESH))
            mem[s][-1].start()

    def build(buf, s, wait):
        def put0(i, _):
            plane0[i, PAD:PAD + lat, :] = buf[s, i, :, :128].astype(F32)
            return 0

        def put1(i, _):
            plane1[i, PAD:PAD + lat, :] = jnp.concatenate(
                [buf[s, i, :, 128:].astype(F32), buf[s, i + half, :, 128:].astype(F32)], axis=-1)
            return 0
        lax.fori_loop(3, lon + 3, put0, 0)
        lax.fori_loop(3, half + 3, put1, 0)
        wait()
        for lo in (0, lon + 3):
            lax.fori_loop(lo, lo + 3, put0, 0)
        for lo in (0, half + 3):
            lax.fori_loop(lo, lo + 3, put1, 0)

    def conv_group(plane, p_id, first, flip):
        acc = [None] * GROUP
        for p in range(7):
            for r in range(GROUP + 6):
                v = plane[first + r, pl.ds(PAD - 3 + p, lat), :].reshape(lat // 8, 8, 128)
                for q in range(7):
                    o = r - q
                    if 0 <= o < GROUP:
                        n = (6 - p) * 7 + (6 - q) if flip else p * 7 + q
                        term = kbr[p_id, n][None] * v
                        acc[o] = term if acc[o] is None else acc[o] + term
        return jnp.concatenate([a.reshape(lat, 128) for a in acc], axis=0)

    def conv(i0, flip, to):
        hbuf[to, :rows, :128] = conv_group(plane0, 0, i0, flip)
        hbuf[to, rows:, :128] = conv_group(plane0, 0, half + i0, flip)
        both = conv_group(plane1, 1, i0, flip)
        hbuf[to, :rows, 128:] = both[:, :rest]
        hbuf[to, rows:, 128:] = both[:, rest:]

    def at_turn(k):
        return lax.rem(k * (blocks - 1), blocks) * GROUP

    def current(i0):
        return jnp.concatenate(
            [cur[pl.ds(i0, GROUP)].reshape(rows, chan), cur[pl.ds(half + i0, GROUP)].reshape(rows, chan)], axis=0)

    blocks = half // GROUP
    for s in range(steps):
        def wait_x(s=s):
            for c in halos[s]:
                c.wait()
        build(xb, s, wait_x)
        back = halo_copies(ahb, s, steps + s)

        def point(k, hidden, s=s):
            i0 = at_turn(k)
            centred = hidden - jnp.mean(hidden, axis=-1, keepdims=True)
            inv_std = lax.rsqrt(jnp.mean(centred * centred, axis=-1, keepdims=True) + norm_eps)
            unit = centred * inv_std
            normed = (unit * gain_ref[...]).astype(BF16)
            bias = jnp.concatenate([bias_ref[n:n + 1] for n in range(bias_ref.shape[0])], axis=-1)
            pre = jnp.dot(normed, up_ref[...], preferred_element_type=F32) + bias
            act = jnp.dot(current(i0), downt[...], preferred_element_type=F32)
            adj_pre = (act * gelu_slope(pre)).astype(BF16)
            scaled = jnp.dot(adj_pre, upt[...], preferred_element_type=F32) * gain_ref[...]
            ah = inv_std * (
                scaled - jnp.mean(scaled, axis=-1, keepdims=True)
                - unit * jnp.mean(scaled * unit, axis=-1, keepdims=True))
            ah = ah.astype(BF16)
            ahb[s, pl.ds(3 + i0, GROUP)] = ah[:rows].reshape(GROUP, lat, chan)
            ahb[s, pl.ds(3 + half + i0, GROUP)] = ah[rows:].reshape(GROUP, lat, chan)

        def both_parts(k, _, back=back, point=point):
            hidden = hbuf[lax.rem(k, 2)]
            conv(at_turn(k + 1), False, lax.rem(k + 1, 2))
            point(k, hidden)

            @pl.when(k == 1)
            def _():
                for c in back:
                    c.start()
            return 0
        conv(at_turn(0), False, 0)
        lax.fori_loop(0, blocks - 1, both_parts, 0)
        point(blocks - 1, hbuf[(blocks - 1) % 2])

        for c in mem[s]:
            c.wait()
        meta, place = places(s)
        total = squares = None
        for i in range(members):
            v = samp[i, s].astype(F32)
            total = v if total is None else total + v
            squares = v * v if squares is None else squares + v * v
        mean = total / members
        var = squares / members - mean * mean
        own = samp[pl.ds(m, 1), s].astype(F32).reshape(slots, chan)
        value = orecv[:, s, :, :chan].astype(F32).reshape(slots, chan)
        ratio = (own - value) / (meta[:, rest + 2:rest + 3] + var)
        dep[s] = jnp.where(meta[:, rest + 3:rest + 4] > 0.5, ratio, 0.0).astype(BF16)

        def wait_back(back=back):
            for c in back:
                c.wait()
        build(ahb, s, wait_back)
        line = jnp.broadcast_to(place, (slots, 128)).T[0:1, :]

        def spread(k, _, s=s, line=line):
            i0 = k * GROUP
            conv(i0, True, 0)
            back_out = hbuf[0]
            row = lax.broadcasted_iota(jnp.int32, (2 * rows, slots), 0)
            row = jnp.where(row < rows, row, row + (half * lat - rows)) + i0 * lat
            hit = jnp.where(row.astype(F32) == line, 1.0, 0.0).astype(BF16)
            forcing = jnp.dot(hit, dep[s], preferred_element_type=F32)
            new = current(i0).astype(F32) + back_out + forcing
            if s < steps - 1:
                new = new.astype(BF16)
                cur[pl.ds(i0, GROUP)] = new[:rows].reshape(GROUP, lat, chan)
                cur[pl.ds(half + i0, GROUP)] = new[rows:].reshape(GROUP, lat, chan)
            else:
                for g in range(2 * GROUP):
                    at = (i0 + (g // GROUP) * half + g % GROUP) * pitch
                    part = new[g * lat:(g + 1) * lat]
                    turn[0, pl.ds(at, lat), :] = part[:, :128]
                    turn[1, pl.ds(at, lat), :rest] = part[:, 128:]
            return 0
        lax.fori_loop(0, blocks, spread, 0)

    for i in range(lat):
        out_ref[i, :, :128] = turn[0, pl.ds(i, lon, stride=pitch), :].astype(BF16)
        out_ref[i, :, 128:] = turn[1, pl.ds(i, lon, stride=pitch), :][:, :rest].astype(BF16)


def per_device(
    adjoint_final, states, kernel_w, norm_gain, up_weight, up_bias, down_weight,
    obs_cell, obs_count, obs_value, obs_error,
):
    tiles, members = lax.axis_size("tile"), lax.axis_size("member")
    steps, _, lat, lon, chan = states.shape
    hid, cap = up_weight.shape[1], obs_cell.shape[3]
    band = lat // tiles
    cell = obs_cell[:, 0]
    slot = jnp.arange(cap, dtype=jnp.int32)
    meta = jnp.stack([
        (cell % lon).astype(BF16),
        (cell // lon + lax.axis_index("tile") * band).astype(BF16),
        obs_error[:, 0],
        (slot < obs_count[:, 0][..., None]).astype(BF16)], axis=-1)
    meta = jnp.pad(meta, ((0, 0),) * 3 + ((0, 256 - chan - 4),))
    slots = tiles * cap
    pitch = lat + 1
    vm = pl.BlockSpec(memory_space=pltpu.VMEM)
    out = pl.pallas_call(
        functools.partial(kernel, tiles, members),
        out_shape=jax.ShapeDtypeStruct((lat, lon, chan), BF16),
        in_specs=[pl.BlockSpec(memory_space=pltpu.HBM)] * 8 + [vm],
        out_specs=vm,
        scratch_shapes=[
            pltpu.VMEM((lat, lon, chan), BF16),
            pltpu.VMEM((steps, lat, lon, chan), BF16),
            pltpu.VMEM((7, 7, chan), F32),
            pltpu.VMEM((1, chan), F32),
            pltpu.VMEM((chan, hid), BF16),
            pltpu.VMEM((hid // 128, 128), F32),
            pltpu.VMEM((chan, hid), BF16),
            pltpu.VMEM((steps, tiles, cap, chan), BF16),
            pltpu.VMEM((tiles, steps, cap, 256), BF16),
            pltpu.VMEM((steps, lon + 6, lat, chan), BF16),
            pltpu.VMEM((steps, lon + 6, lat, chan), BF16),
            pltpu.VMEM((lon, lat, chan), BF16),
            pltpu.VMEM((lon + 6, lat + 2 * PAD, 128), F32),
            pltpu.VMEM((lon // 2 + 6, lat + 2 * PAD, 128), F32),
            pltpu.VMEM((2, 49, 8, 128), F32),
            pltpu.VMEM((2, 2 * GROUP * lat, chan), F32),
            pltpu.VMEM((2, pitch * lon, 128), F32),
            pltpu.VMEM((hid, chan), BF16),
            pltpu.VMEM((tiles, steps, cap, 256), BF16),
            pltpu.VMEM((members, steps, slots, chan), BF16),
            pltpu.VMEM((steps, slots, chan), BF16),
            pltpu.SemaphoreType.DMA((steps + 7,)),
            pltpu.SemaphoreType.DMA((tiles,)),
            pltpu.SemaphoreType.DMA((tiles,)),
            pltpu.SemaphoreType.DMA((steps, members)),
            pltpu.SemaphoreType.DMA((steps, members)),
            pltpu.SemaphoreType.DMA((2 * steps, 2)),
            pltpu.SemaphoreType.DMA((2 * steps, 2)),
        ],
        compiler_params=pltpu.CompilerParams(
            collective_id=0, has_side_effects=True, vmem_limit_bytes=127 * 512 * 1024),
    )(
        adjoint_final[0], states[:, 0], kernel_w, norm_gain.reshape(1, chan),
        up_weight, up_bias.reshape(hid // 128, 128), down_weight.T, obs_value[:, 0], meta,
    )
    return out[None]


def solution(mesh):
    placed = (
        P("member", None, "tile", None),
        P(None, "member", None, "tile", None),
        P(), P(), P(), P(), P(),
        P(None, "tile", None, None),
        P(None, "tile", None),
        P(None, "tile", None, None, None),
        P(None, "tile", None, None),
    )
    return jax.shard_map(
        per_device, mesh=mesh, in_specs=placed, out_specs=P("member", None, "tile", None), check_vma=False)
```

```python
import functools
import math

import jax
import jax.numpy as jnp
from jax import lax
from jax.experimental import pallas as pl
from jax.experimental.pallas import tpu as pltpu
from jax.sharding import PartitionSpec as P

slope_coef = math.sqrt(2.0 / math.pi)
cubic_coef = 0.044715
norm_eps = 1e-06
MESH = pl.DeviceIdType.MESH
F32, BF16 = jnp.float32, jnp.bfloat16
GROUP = 4


def gelu_slope(u):
    u2 = u * u
    w = jnp.tanh(u * (slope_coef + (slope_coef * cubic_coef) * u2))
    outer = u * (0.5 * slope_coef + (1.5 * slope_coef * cubic_coef) * u2)
    return (0.5 + 0.5 * w) + (1.0 - w * w) * outer


def kernel(
    tiles, members, adj_ref, st_ref, kern_ref, gain_ref, up_ref, bias_ref, downt, obs_ref, meta_ref, out_ref,
    pack_ref, xb, ahb, cur, plane1, kbr, hbuf, turn, upt, orecv, samp, dep,
    obs_send, obs_recv, mem_send, mem_recv, halo_send, halo_recv,
):
    steps, lat, lon, chan = st_ref.shape
    half, cells, slots = lon // 2, lat * lon, tiles * pack_ref.shape[2]
    rest = chan - 128
    pitch = turn.shape[1] // lon
    rows = GROUP * lat
    t, m = lax.axis_index("tile"), lax.axis_index("member")

    barrier = pltpu.get_barrier_semaphore()
    for d in range(1, tiles):
        pl.semaphore_signal(barrier, inc=1, device_id={"tile": lax.rem(t + d, tiles)}, device_id_type=MESH)
    for d in range(1, members):
        pl.semaphore_signal(barrier, inc=1, device_id={"member": lax.rem(m + d, members)}, device_id_type=MESH)

    def to_lon_major(load, store):
        for i in range(lat):
            v = load(i).astype(F32)
            turn[0, pl.ds(i * pitch, lon), :] = v[:, :128]
            turn[1, pl.ds(i * pitch, lon), :rest] = v[:, 128:]
        for k in range(lon):
            a = turn[0, pl.ds(k, lat, stride=pitch), :]
            b = turn[1, pl.ds(k, lat, stride=pitch), :]
            store(k, a, b[:, :rest])

    def halo_copies(buf, s, n):
        right, left = lax.rem(t + 1, tiles), lax.rem(t + tiles - 1, tiles)
        out = []
        for d, (src, dst, to) in enumerate(((lon, 0, right), (3, lon + 3, left))):
            out.append(pltpu.make_async_remote_copy(
                src_ref=buf.at[s, pl.ds(src, 3)], dst_ref=buf.at[s, pl.ds(dst, 3)],
                send_sem=halo_send.at[n, d], recv_sem=halo_recv.at[n, d],
                device_id={"tile": to}, device_id_type=MESH))
        return out

    def turn_state(s):
        def store_x(k, a, b):
            xb[s, 3 + k, :, :128] = a.astype(BF16)
            xb[s, 3 + k, :, 128:] = b.astype(BF16)
        to_lon_major(lambda i: st_ref[s, i], store_x)

    for s in range(steps):
        pack_ref[:, s, :, :chan] = obs_ref[s]
        pack_ref[:, s, :, chan:] = meta_ref[s]
    orecv[pl.ds(t, 1)] = pack_ref[pl.ds(t, 1)]
    turn_state(0)

    pl.semaphore_wait(barrier, tiles - 1 + members - 1)
    obs = []
    for d in range(1, tiles):
        to = lax.rem(t + d, tiles)
        obs.append(pltpu.make_async_remote_copy(
            src_ref=pack_ref.at[to], dst_ref=orecv.at[t], send_sem=obs_send.at[d], recv_sem=obs_recv.at[d],
            device_id={"tile": to}, device_id_type=MESH))
        obs[-1].start()
    halos = [halo_copies(xb, s, s) for s in range(steps)]
    for s in range(steps):
        if s > 0:
            turn_state(s)
        for c in halos[s]:
            c.start()

    def store_adj(k, a, b):
        cur[k, :, :128] = a.astype(BF16)
        cur[k, :, 128:] = b.astype(BF16)
    to_lon_major(lambda i: adj_ref[i], store_adj)
    upt[...] = up_ref[...].T
    for n in range(49):
        taps = kern_ref[n // 7, n % 7:n % 7 + 1, :]
        kbr[0, n] = jnp.broadcast_to(taps[:, :128], (16, 128)).astype(BF16)
        tail = jnp.broadcast_to(taps[:, 128:], (16, rest)).astype(BF16)
        kbr[1, n, :, :rest] = tail
        kbr[1, n, :, rest:] = tail
    for c in obs:
        c.wait()

    def places(s):
        meta = orecv[:, s, :, 128:].astype(F32).reshape(slots, 128)
        lon_at, lat_at = meta[:, rest:rest + 1], meta[:, rest + 1:rest + 2]
        return meta, lon_at * lat + lat_at

    mem = []
    for s in range(steps):
        _, place = places(s)
        ids = lax.broadcasted_iota(jnp.int32, (slots, cells), 1).astype(F32)
        pick = jnp.where(ids == place, 1.0, 0.0).astype(BF16)
        got = jnp.dot(pick, xb[s, 3:3 + lon].reshape(cells, chan), preferred_element_type=F32)
        samp[pl.ds(m, 1), s] = got.astype(BF16).reshape(1, slots, chan)
        mem.append([])
        for d in range(1, members):
            mem[s].append(pltpu.make_async_remote_copy(
                src_ref=samp.at[m, s], dst_ref=samp.at[m, s], send_sem=mem_send.at[s, d], recv_sem=mem_recv.at[s, d],
                device_id={"member": lax.rem(m + d, members)}, device_id_type=MESH))
            mem[s][-1].start()

    def build(buf, s, wait):
        def put1(i, _):
            plane1[i] = jnp.concatenate(
                [buf[s, i, :, 128:].astype(F32), buf[s, i + half, :, 128:].astype(F32)], axis=-1).astype(BF16)
            return 0
        lax.fori_loop(3, half + 3, put1, 0)
        wait()
        for lo in (0, half + 3):
            lax.fori_loop(lo, lo + 3, put1, 0)

    def conv_group(load, p_id, flip):
        views = [load(r).reshape(lat // 16, 16, 128) for r in range(GROUP + 6)]
        line_at = lax.broadcasted_iota(jnp.int32, (lat, 128), 0)
        acc = [None] * GROUP
        for p in range(7):
            shift = p - 3
            taps = [kbr[p_id, (6 - p) * 7 + (6 - q) if flip else p * 7 + q][None] for q in range(7)]
            for o in range(GROUP):
                t = [taps[q] * views[o + q] for q in range(7)]
                part = ((t[0] + t[1]) + (t[2] + t[3])) + ((t[4] + t[5]) + t[6])
                part = part.reshape(lat, 128).astype(F32)
                if shift:
                    part = pltpu.roll(part, (-shift) % lat, 0)
                    inside = line_at < lat - shift if shift > 0 else line_at >= -shift
                    part = jnp.where(inside, part, 0.0)
                acc[o] = part if acc[o] is None else acc[o] + part
        return jnp.concatenate(acc, axis=0)

    def conv(buf, s, i0, flip, to):
        hbuf[to, :rows, :128] = conv_group(lambda r: buf[s, i0 + r, :, :128], 0, flip)
        hbuf[to, rows:, :128] = conv_group(lambda r: buf[s, half + i0 + r, :, :128], 0, flip)
        both = conv_group(lambda r: plane1[i0 + r], 1, flip)
        hbuf[to, :rows, 128:] = both[:, :rest]
        hbuf[to, rows:, 128:] = both[:, rest:]

    def at_turn(k):
        return lax.rem(k * (blocks - 1), blocks) * GROUP

    def current(i0):
        return jnp.concatenate(
            [cur[pl.ds(i0, GROUP)].reshape(rows, chan), cur[pl.ds(half + i0, GROUP)].reshape(rows, chan)], axis=0)

    blocks = half // GROUP
    for s in range(steps):
        def wait_x(s=s):
            for c in halos[s]:
                c.wait()
        build(xb, s, wait_x)
        back = halo_copies(ahb, s, steps + s)

        def point(k, hidden, s=s):
            i0 = at_turn(k)
            centred = hidden - jnp.mean(hidden, axis=-1, keepdims=True)
            inv_std = lax.rsqrt(jnp.mean(centred * centred, axis=-1, keepdims=True) + norm_eps)
            unit = centred * inv_std
            normed = (unit * gain_ref[...]).astype(BF16)
            bias = jnp.concatenate([bias_ref[n:n + 1] for n in range(bias_ref.shape[0])], axis=-1)
            pre = jnp.dot(normed, up_ref[...], preferred_element_type=F32) + bias
            act = jnp.dot(current(i0), downt[...], preferred_element_type=F32)
            adj_pre = (act * gelu_slope(pre)).astype(BF16)
            scaled = jnp.dot(adj_pre, upt[...], preferred_element_type=F32) * gain_ref[...]
            ah = inv_std * (
                scaled - jnp.mean(scaled, axis=-1, keepdims=True)
                - unit * jnp.mean(scaled * unit, axis=-1, keepdims=True))
            ah = ah.astype(BF16)
            ahb[s, pl.ds(3 + i0, GROUP)] = ah[:rows].reshape(GROUP, lat, chan)
            ahb[s, pl.ds(3 + half + i0, GROUP)] = ah[rows:].reshape(GROUP, lat, chan)

        def both_parts(k, _, s=s, back=back, point=point):
            conv(xb, s, at_turn(k), False, 0)
            point(k, hbuf[0])

            @pl.when(k == 1)
            def _():
                for c in back:
                    c.start()
            return 0
        lax.fori_loop(0, blocks, both_parts, 0)

        for c in mem[s]:
            c.wait()
        meta, place = places(s)
        total = squares = None
        for i in range(members):
            v = samp[i, s].astype(F32)
            total = v if total is None else total + v
            squares = v * v if squares is None else squares + v * v
        mean = total / members
        var = squares / members - mean * mean
        own = samp[pl.ds(m, 1), s].astype(F32).reshape(slots, chan)
        value = orecv[:, s, :, :chan].astype(F32).reshape(slots, chan)
        ratio = (own - value) / (meta[:, rest + 2:rest + 3] + var)
        dep[s] = jnp.where(meta[:, rest + 3:rest + 4] > 0.5, ratio, 0.0).astype(BF16)

        def wait_back(back=back):
            for c in back:
                c.wait()
        build(ahb, s, wait_back)
        line = jnp.broadcast_to(place, (slots, 128)).T[0:1, :]

        def spread(k, _, s=s, line=line):
            i0 = k * GROUP
            conv(ahb, s, i0, True, 0)
            back_out = hbuf[0]
            row = lax.broadcasted_iota(jnp.int32, (2 * rows, slots), 0)
            row = jnp.where(row < rows, row, row + (half * lat - rows)) + i0 * lat
            hit = jnp.where(row.astype(F32) == line, 1.0, 0.0).astype(BF16)
            forcing = jnp.dot(hit, dep[s], preferred_element_type=F32)
            new = current(i0).astype(F32) + back_out + forcing
            if s < steps - 1:
                new = new.astype(BF16)
                cur[pl.ds(i0, GROUP)] = new[:rows].reshape(GROUP, lat, chan)
                cur[pl.ds(half + i0, GROUP)] = new[rows:].reshape(GROUP, lat, chan)
            else:
                for g in range(2 * GROUP):
                    at = (i0 + (g // GROUP) * half + g % GROUP) * pitch
                    part = new[g * lat:(g + 1) * lat]
                    turn[0, pl.ds(at, lat), :] = part[:, :128]
                    turn[1, pl.ds(at, lat), :rest] = part[:, 128:]
            return 0
        lax.fori_loop(0, blocks, spread, 0)

    for i in range(lat):
        out_ref[i, :, :128] = turn[0, pl.ds(i, lon, stride=pitch), :].astype(BF16)
        out_ref[i, :, 128:] = turn[1, pl.ds(i, lon, stride=pitch), :][:, :rest].astype(BF16)


def per_device(
    adjoint_final, states, kernel_w, norm_gain, up_weight, up_bias, down_weight,
    obs_cell, obs_count, obs_value, obs_error,
):
    tiles, members = lax.axis_size("tile"), lax.axis_size("member")
    steps, _, lat, lon, chan = states.shape
    hid, cap = up_weight.shape[1], obs_cell.shape[3]
    band = lat // tiles
    cell = obs_cell[:, 0]
    slot = jnp.arange(cap, dtype=jnp.int32)
    meta = jnp.stack([
        (cell % lon).astype(BF16),
        (cell // lon + lax.axis_index("tile") * band).astype(BF16),
        obs_error[:, 0],
        (slot < obs_count[:, 0][..., None]).astype(BF16)], axis=-1)
    meta = jnp.pad(meta, ((0, 0),) * 3 + ((0, 256 - chan - 4),))
    slots = tiles * cap
    pitch = lat + 1
    vm = pl.BlockSpec(memory_space=pltpu.VMEM)
    out = pl.pallas_call(
        functools.partial(kernel, tiles, members),
        out_shape=jax.ShapeDtypeStruct((lat, lon, chan), BF16),
        in_specs=[vm] * 9,
        out_specs=vm,
        scratch_shapes=[
            pltpu.VMEM((tiles, steps, cap, 256), BF16),
            pltpu.VMEM((steps, lon + 6, lat, chan), BF16),
            pltpu.VMEM((steps, lon + 6, lat, chan), BF16),
            pltpu.VMEM((lon, lat, chan), BF16),
            pltpu.VMEM((lon // 2 + 6, lat, 128), BF16),
            pltpu.VMEM((2, 49, 16, 128), BF16),
            pltpu.VMEM((1, 2 * GROUP * lat, chan), F32),
            pltpu.VMEM((2, pitch * lon, 128), F32),
            pltpu.VMEM((hid, chan), BF16),
            pltpu.VMEM((tiles, steps, cap, 256), BF16),
            pltpu.VMEM((members, steps, slots, chan), BF16),
            pltpu.VMEM((steps, slots, chan), BF16),
            pltpu.SemaphoreType.DMA((tiles,)),
            pltpu.SemaphoreType.DMA((tiles,)),
            pltpu.SemaphoreType.DMA((steps, members)),
            pltpu.SemaphoreType.DMA((steps, members)),
            pltpu.SemaphoreType.DMA((2 * steps, 2)),
            pltpu.SemaphoreType.DMA((2 * steps, 2)),
        ],
        compiler_params=pltpu.CompilerParams(
            collective_id=0, has_side_effects=True, vmem_limit_bytes=48 * 1024 * 1024),
    )(
        adjoint_final[0], states[:, 0], kernel_w, norm_gain.reshape(1, chan),
        up_weight, up_bias.reshape(hid // 128, 128), down_weight.T, obs_value[:, 0], meta,
    )
    return out[None]


def solution(mesh):
    placed = (
        P("member", None, "tile", None),
        P(None, "member", None, "tile", None),
        P(), P(), P(), P(), P(),
        P(None, "tile", None, None),
        P(None, "tile", None),
        P(None, "tile", None, None, None),
        P(None, "tile", None, None),
    )
    return jax.shard_map(
        per_device, mesh=mesh, in_specs=placed, out_specs=P("member", None, "tile", None), check_vma=False)
```
